32 devices in a mesh: dp: 8 (over z, y), rows: 4 (over x, core).
Axes of the slice: x: 2, y: 2, z: 4, core: 2. Of those that a mesh axis runs over, the one named last changes fastest.
Arguments:
- images: bfloat16 [8, 48, 64, 256], P('dp', 'rows'), may hold values from -6 to 6
- kernel: bfloat16 [3, 3, 256, 256], replicated, may hold values from -0.125 to 0.125
- cotangent: bfloat16 [8, 48, 64, 256], P('dp', 'rows'), may hold values from -6 to 6
Outputs:
- output_maps: bfloat16 [8, 48, 64, 256], P('dp', 'rows')
- grad_input: bfloat16 [8, 48, 64, 256], P('dp', 'rows')
- grad_kernel: float32 [3, 3, 256, 256], P(None, None, None, 'rows')
The draws below stay inside these ranges and needn't reach their ends.
All inputs are finite; a program needn't handle non-finite values.
Results may differ from the reference program's by a relative error of at most 0.001.
Values may be sent and summed in bfloat16 or wider, within the bound.
A program may use at most 64 MiB of HBM per device.

```python
import jax
import jax.numpy as jnp
from jax import lax

CHANNELS = 256
COLS = 64
BATCH = 8
HEIGHT = 48


def spiked(result, key, source, target, blocks, factor):
    def block_of(axis_at):
        return (jnp.arange(result.shape[axis_at]) // (result.shape[axis_at] // blocks)).reshape((-1,) + (1,) * (result.ndim - 1 - axis_at))

    near = jax.random.permutation(key, blocks)[block_of(target)]
    second = (block_of(target) + blocks // 2) % blocks
    return jnp.where((block_of(source) == near) | (block_of(source) == second), factor * result, result)


def block_scale(own_key, shape, pieces, smallest, high):
    loudness = 1.0
    for axis_at, parts in pieces:
        heights = jax.random.uniform(jax.random.fold_in(jax.random.fold_in(own_key, 6), axis_at), (parts,), jnp.float32, smallest / len(pieces), high / len(pieces))
        loudness = loudness * jnp.repeat(jnp.exp(heights), shape[axis_at] // parts).reshape((-1,) + (1,) * (len(shape) - 1 - axis_at))
    return loudness


def normal_values(rng, extent, scale, most, cuts=(), kind=jnp.bfloat16):
    entries = scale * jax.random.normal(rng, extent, jnp.float32)
    if cuts:
        entries = entries * block_scale(rng, extent, cuts, -0.22, 0.18)
    return jnp.clip(entries, -most, most).astype(kind)


def heavy_noise(stream_key, dims, scale, limit, shards, heavy, dtype=jnp.bfloat16):
    array = scale * jax.random.normal(stream_key, dims, jnp.float32)
    if shards:
        array = array * block_scale(stream_key, dims, shards, -0.22, 0.18)
    return jnp.clip(spiked(array, jax.random.fold_in(stream_key, 3), *heavy), -limit, limit).astype(dtype)


def setup_inputs(seed: int = 0) -> dict:
    splits = jax.random.split(jax.random.key(seed), 4)
    return {
        "images": heavy_noise(splits[0], (BATCH, HEIGHT, COLS, CHANNELS), 1.0, 6.0, ((0, 8), (1, 4)), (0, 3, 8, 2.0)),
        "kernel": normal_values(splits[1], (3, 3, CHANNELS, CHANNELS), (9 * CHANNELS) ** -0.5, 0.125),
        "cotangent": heavy_noise(splits[2], (BATCH, HEIGHT, COLS, CHANNELS), 1.0, 6.0, ((0, 8), (1, 4)), (1, 3, 4, 2.0)),
    }


def conv_same(inputs, weights):
    return lax.conv_general_dilated(inputs, weights, (1, 1), ((1, 1), (1, 1)), dimension_numbers=("NHWC", "HWIO", "NHWC"), preferred_element_type=jnp.float32)


def reference(images, kernel, cotangent):
    flipped = jnp.transpose(kernel[::-1, ::-1], (0, 1, 3, 2))

    def sample_step(running, sample_pair):
        sample_image, sample_grad = sample_pair
        forward_maps = conv_same(sample_image[None], kernel)[0].astype(jnp.bfloat16)
        backward_maps = conv_same(sample_grad[None], flipped)[0].astype(jnp.bfloat16)
        padded = jnp.pad(sample_image.astype(jnp.float32), ((1, 1), (1, 1), (0, 0)))
        grad_float = sample_grad.astype(jnp.float32)
        tap_rows = []
        for tap_row in range(3):
            tap_line = []
            for tap_col in range(3):
                window = padded[tap_row:tap_row + HEIGHT, tap_col:tap_col + COLS]
                tap_line.append(jnp.einsum("hwc,hwd->cd", window, grad_float))
            tap_rows.append(jnp.stack(tap_line))
        return running + jnp.stack(tap_rows), (forward_maps, backward_maps)

    start_sum = jnp.zeros((3, 3, CHANNELS, CHANNELS), jnp.float32)
    summed, (forward_all, backward_all) = lax.scan(sample_step, start_sum, (images, cotangent))
    return forward_all, backward_all, summed / float(BATCH)
```

```python
import functools

import jax
import jax.numpy as jnp
from jax import lax
from jax.experimental import pallas as pl
from jax.experimental.pallas import tpu as pltpu
from jax.sharding import PartitionSpec as P

MESH = pl.DeviceIdType.MESH
SUB = 8
TAP_ORDER = (1, 0, 2)


def bits_of(size):
    return size.bit_length() - 1


def plan(rows_size, groups, pieces):
    steps = [("rows", bit, True) for bit in reversed(range(1, bits_of(rows_size)))]
    left = pieces
    for bit in range(bits_of(groups)):
        split = left > 1
        steps.append(("dp", bit, split))
        left = left // 2 if split else left
    return steps


def body(
    dims,
    img_ref, ker_ref, cot_ref,
    out_ref, gin_ref, gk_ref,
    wide_img, wide_cot, cot_t, halo, acc, first, work, fin, *rest,
):
    rows_size, groups, rows_dev, cols, chan, steps = dims
    landing = rest[: len(steps)]
    bar_less = rest[len(steps):]
    halo_send, halo_recv, send_sem, recv_sem = bar_less
    pixels = rows_dev * cols
    pieces = chan // rows_size // SUB
    width = 3 * chan
    r = lax.axis_index("rows")
    g = lax.axis_index("dp")
    right = lax.rem(r + 1, rows_size)
    left = lax.rem(r + rows_size - 1, rows_size)

    def flip(axis, bit):
        me = r if axis == "rows" else g
        mine = lax.rem(me // (1 << bit), 2)
        return mine, {axis: me + (1 - 2 * mine) * (1 << bit)}

    core, core_peer = flip("rows", 0)
    barrier = pltpu.get_barrier_semaphore()
    greeted = [{"rows": right}, {"rows": left}, core_peer]
    greeted += [flip(axis, bit)[1] for axis, bit, _ in steps]
    for peer in greeted:
        pl.semaphore_signal(barrier, inc=1, device_id=peer, device_id_type=MESH)

    column = lax.broadcasted_iota(jnp.int32, (cols, chan), 0)

    def widen(dst, slot, value):
        full = value.astype(jnp.float32)
        before = jnp.where(column == 0, 0.0, pltpu.roll(full, 1, 0))
        after = jnp.where(column == cols - 1, 0.0, pltpu.roll(full, cols - 1, 0))
        at = pl.ds(pl.multiple_of(slot * cols, cols), cols)
        dst[at, 0:chan] = before.astype(jnp.bfloat16)
        dst[at, chan : 2 * chan] = value
        dst[at, 2 * chan :] = after.astype(jnp.bfloat16)

    def widen_rows(dst, src):
        def one(i, carry):
            widen(dst, i + 1, src[pl.ds(pl.multiple_of(i * cols, cols), cols), :])
            return carry

        lax.fori_loop(0, rows_dev, one, 0)

    pl.semaphore_wait(barrier, len(greeted))
    halos = []
    for k, (src, at, to) in enumerate((
        (img_ref, pixels - cols, right), (img_ref, 0, left),
        (cot_ref, pixels - cols, right), (cot_ref, 0, left),
    )):
        halos.append(pltpu.make_async_remote_copy(
            src_ref=src.at[pl.ds(at, cols)], dst_ref=halo.at[k],
            send_sem=halo_send.at[k], recv_sem=halo_recv.at[k],
            device_id={"rows": to}, device_id_type=MESH,
        ))
        halos[-1].start()

    cot_t[...] = jnp.transpose(cot_ref[...])
    widen_rows(wide_img, img_ref)

    def edges(dst, k):
        halos[k].wait_recv()
        halos[k + 1].wait_recv()
        zero = jnp.zeros((cols, chan), jnp.bfloat16)
        widen(dst, 0, jnp.where(r > 0, halo[k], zero))
        widen(dst, rows_dev + 1, jnp.where(r < rows_size - 1, halo[k + 1], zero))

    sent = []

    def send(src, dst, c, k, peer):
        copy = pltpu.make_async_remote_copy(
            src_ref=src, dst_ref=dst, send_sem=send_sem.at[c, k],
            recv_sem=recv_sem.at[c, k], device_id=peer, device_id_type=MESH,
        )
        copy.start()
        return copy

    def chunk(c):
        tap = TAP_ORDER[c]
        for b in range(3):
            part = jnp.dot(
                cot_t[...],
                wide_img[tap * cols : tap * cols + pixels, b * chan : (b + 1) * chan],
                preferred_element_type=jnp.float32,
            )
            acc[c, :, :, :, :, b * chan : (b + 1) * chan] = part.reshape(
                rows_size // 2, 2, pieces, SUB, chan)
        copy = send(acc.at[c, :, 1 - core], first.at[c], c, 0, core_peer)
        sent.append(copy)
        yield
        copy.wait_recv()
        work[c] = acc[c, :, core] + first[c]
        q0, nq, p0, np_ = 0, rows_size // 2, 0, pieces
        undo = []
        for k, (axis, bit, split) in enumerate(steps):
            mine, peer = flip(axis, bit)
            sq, sp = q0, p0
            if axis == "rows":
                nq //= 2
                q0, sq = q0 + mine * nq, q0 + (1 - mine) * nq
            elif split:
                np_ //= 2
                p0, sp = p0 + mine * np_, p0 + (1 - mine) * np_
                undo.append((mine, peer))
            copy = send(
                work.at[c, pl.ds(sq, nq), pl.ds(sp, np_)], landing[k].at[c], c, k + 1, peer)
            yield
            copy.wait_recv()
            if axis == "dp" and not split:
                copy.wait_send()
            else:
                sent.append(copy)
            keep = (c, pl.ds(q0, nq), pl.ds(p0, np_))
            work[keep] = work[keep] + landing[k][c]
        fin[c, pl.ds(p0, np_)] = work[c, q0, pl.ds(p0, np_)]
        for k, (mine, peer) in enumerate(reversed(undo)):
            at = fin.at[c, pl.ds(p0, np_)]
            copy = send(at, at, c, 1 + len(steps) + k, peer)
            sent.append(copy)
            yield
            copy.wait_recv()
            p0 = p0 - mine * np_
            np_ *= 2
        gk_ref[tap] = fin[c].reshape(pieces * SUB, width)

    def forward_maps():
        block = 4 * cols if rows_dev % 4 == 0 else cols

        def one(m, carry):
            total = jnp.zeros((block, chan), jnp.float32)
            for a in range(3):
                at = pl.ds(pl.multiple_of(m * block + a * cols, cols), block)
                total += jnp.dot(wide_img[at, :], ker_ref[a], preferred_element_type=jnp.float32)
            out_ref[pl.ds(pl.multiple_of(m * block, block), block), :] = total.astype(jnp.bfloat16)
            return carry

        lax.fori_loop(0, pixels // block, one, 0)

    def backward_maps():
        block = 4 * cols if rows_dev % 4 == 0 else cols

        def one(m, carry):
            total = jnp.zeros((block, chan), jnp.float32)
            for a in range(3):
                at = pl.ds(pl.multiple_of(m * block + a * cols, cols), block)
                for b in range(3):
                    total += lax.dot_general(
                        wide_cot[at, b * chan : (b + 1) * chan],
                        ker_ref[2 - a, (2 - b) * chan : (3 - b) * chan, :],
                        (((1,), (1,)), ((), ())),
                        preferred_element_type=jnp.float32,
                    )
            gin_ref[pl.ds(pl.multiple_of(m * block, block), block), :] = total.astype(jnp.bfloat16)
            return carry

        lax.fori_loop(0, pixels // block, one, 0)

    chunks = [chunk(c) for c in range(3)]
    next(chunks[0])
    edges(wide_img, 0)
    next(chunks[1])
    next(chunks[2])
    for one in chunks:
        next(one)
    forward_maps()
    next(chunks[0])
    widen_rows(wide_cot, cot_ref)
    edges(wide_cot, 2)
    backward_maps()
    next(chunks[1])
    live = chunks
    while live:
        still = []
        for one in live:
            if next(one, live) is not live:
                still.append(one)
        live = still
    for copy in halos + sent:
        copy.wait_send()


def shards(images, kernel, cotangent):
    rows_size, groups = lax.axis_size("rows"), lax.axis_size("dp")
    batch, rows_dev, cols, chan = images.shape
    pixels = rows_dev * cols
    share = chan // rows_size
    pieces = share // SUB
    width = 3 * chan
    steps = plan(rows_size, groups, pieces)
    landing = []
    nq, np_ = rows_size // 2, pieces
    for axis, _, split in steps:
        if axis == "rows":
            nq //= 2
        elif split:
            np_ //= 2
        landing.append(pltpu.VMEM((3, nq, np_, SUB, width), jnp.float32))
    count = 1 + len(steps) + sum(1 for axis, _, split in steps if axis == "dp" and split)
    vmem = pl.BlockSpec(memory_space=pltpu.VMEM)
    out, gin, gk = pl.pallas_call(
        functools.partial(body, (rows_size, groups, rows_dev, cols, chan, steps)),
        out_shape=(
            jax.ShapeDtypeStruct((pixels, chan), jnp.bfloat16),
            jax.ShapeDtypeStruct((pixels, chan), jnp.bfloat16),
            jax.ShapeDtypeStruct((3, share, width), jnp.float32),
        ),
        in_specs=[vmem] * 3,
        out_specs=(vmem,) * 3,
        scratch_shapes=[
            pltpu.VMEM(((rows_dev + 2) * cols, width), jnp.bfloat16),
            pltpu.VMEM(((rows_dev + 2) * cols, width), jnp.bfloat16),
            pltpu.VMEM((chan, pixels), jnp.bfloat16),
            pltpu.VMEM((4, cols, chan), jnp.bfloat16),
            pltpu.VMEM((3, rows_size // 2, 2, pieces, SUB, width), jnp.float32),
            pltpu.VMEM((3, rows_size // 2, pieces, SUB, width), jnp.float32),
            pltpu.VMEM((3, rows_size // 2, pieces, SUB, width), jnp.float32),
            pltpu.VMEM((3, pieces, SUB, width), jnp.float32),
            *landing,
            pltpu.SemaphoreType.DMA((4,)),
            pltpu.SemaphoreType.DMA((4,)),
            pltpu.SemaphoreType.DMA((3, count)),
            pltpu.SemaphoreType.DMA((3, count)),
        ],
        compiler_params=pltpu.CompilerParams(
            collective_id=0, has_side_effects=True, vmem_limit_bytes=40 * 2**20),
        cost_estimate=pl.CostEstimate(
            flops=6 * 9 * pixels * chan * chan, bytes_accessed=6 * 2**20, transcendentals=0),
    )(
        images.reshape(pixels, chan),
        kernel.reshape(3, 3 * chan, chan),
        cotangent.reshape(pixels, chan),
    )
    summed = jnp.transpose(gk.reshape(3, share, 3, chan), (0, 2, 3, 1))
    batch_total = batch * groups
    return (out.reshape(images.shape), gin.reshape(images.shape), summed / float(batch_total))


def solution(mesh):
    return jax.shard_map(
        shards,
        mesh=mesh,
        in_specs=(P("dp", "rows", None, None), P(), P("dp", "rows", None, None)),
        out_specs=(
            P("dp", "rows", None, None),
            P("dp", "rows", None, None),
            P(None, None, None, "rows"),
        ),
        check_vma=False,
    )
```

```python
import functools

import jax
import jax.numpy as jnp
from jax import lax
from jax.experimental import pallas as pl
from jax.experimental.pallas import tpu as pltpu
from jax.sharding import PartitionSpec as P

MESH = pl.DeviceIdType.MESH
SUB = 8
TAP_ORDER = (1, 0, 2)
GAP = 3


def bits_of(size):
    return size.bit_length() - 1


def plan(rows_size, groups, pieces):
    steps = [("rows", bit, 2, True) for bit in reversed(range(1, bits_of(rows_size)))]
    left, bit = pieces, 0
    while bit < bits_of(groups):
        several = bit > 0 and left % 4 == 0 and bit + 2 <= bits_of(groups)
        members = 4 if several else 2
        split = left % members == 0
        steps.append(("dp", bit, members, split))
        left = left // members if split else left
        bit += bits_of(members)
    return steps


def body(
    dims,
    img_hbm, ker_hbm, cot_hbm,
    out_hbm, gin_hbm, gk_hbm,
    out_ref, gin_ref, img_ref, ker_ref, cot_ref, wide_img, wide_cot, cot_t, halo, acc, first, work, fin, *rest,
):
    rows_size, groups, rows_dev, cols, chan, steps = dims
    landing = rest[: len(steps)]
    load_sem, store_sem, tap_sem, halo_send, halo_recv, send_sem, recv_sem = rest[len(steps):]
    pixels = rows_dev * cols
    pieces = chan // rows_size // SUB
    r = lax.axis_index("rows")
    g = lax.axis_index("dp")
    right = lax.rem(r + 1, rows_size)
    left = lax.rem(r + rows_size - 1, rows_size)

    loads = [
        pltpu.make_async_copy(src, dst, load_sem.at[k])
        for k, (src, dst) in enumerate(
            ((img_hbm, img_ref), (cot_hbm, cot_ref), (ker_hbm, ker_ref)))
    ]
    for load in loads:
        load.start()

    def mates(axis, bit, members):
        me = r if axis == "rows" else g
        mine = lax.rem(me // (1 << bit), members)
        others = []
        for k in range(1, members):
            place = lax.rem(mine + k, members)
            others.append((place, {axis: me + (place - mine) * (1 << bit)}))
        return mine, others

    core, ((_, core_peer),) = mates("rows", 0, 2)
    barrier = pltpu.get_barrier_semaphore()
    greeted = [{"rows": right}, {"rows": left}, core_peer]
    greeted += [peer for step in steps for _, peer in mates(*step[:3])[1]]
    for peer in greeted:
        pl.semaphore_signal(barrier, inc=1, device_id=peer, device_id_type=MESH)

    column = lax.broadcasted_iota(jnp.int32, (cols, chan), 0)

    def widen(dst, slot, value):
        full = value.astype(jnp.float32)
        before = jnp.where(column == 0, 0.0, pltpu.roll(full, 1, 0))
        after = jnp.where(column == cols - 1, 0.0, pltpu.roll(full, cols - 1, 0))
        at = pl.ds(pl.multiple_of(slot * cols, cols), cols)
        dst[at, 0:chan] = before.astype(jnp.bfloat16)
        dst[at, chan : 2 * chan] = value
        dst[at, 2 * chan :] = after.astype(jnp.bfloat16)

    def widen_rows(dst, src):
        def one(i, carry):
            widen(dst, i + 1, src[pl.ds(pl.multiple_of(i * cols, cols), cols), :])
            return carry

        lax.fori_loop(0, rows_dev, one, 0)

    loads[0].wait()
    widen_rows(wide_img, img_ref)
    loads[1].wait()
    cot_t[...] = jnp.transpose(cot_ref[...])

    pl.semaphore_wait(barrier, len(greeted))
    halos = []
    for k, (src, at, to) in enumerate((
        (img_ref, pixels - cols, right), (img_ref, 0, left),
        (cot_ref, pixels - cols, right), (cot_ref, 0, left),
    )):
        halos.append(pltpu.make_async_remote_copy(
            src_ref=src.at[pl.ds(at, cols)], dst_ref=halo.at[k],
            send_sem=halo_send.at[k], recv_sem=halo_recv.at[k],
            device_id={"rows": to}, device_id_type=MESH,
        ))
        halos[-1].start()

    def edges(dst, k):
        halos[k].wait_recv()
        halos[k + 1].wait_recv()
        zero = jnp.zeros((cols, chan), jnp.bfloat16)
        widen(dst, 0, jnp.where(r > 0, halo[k], zero))
        widen(dst, rows_dev + 1, jnp.where(r < rows_size - 1, halo[k + 1], zero))

    sent, stores = [], []

    def store(src, dst, sem):
        stores.append(pltpu.make_async_copy(src, dst, sem))
        stores[-1].start()

    def send(src, dst, c, k, peer):
        copy = pltpu.make_async_remote_copy(
            src_ref=src, dst_ref=dst, send_sem=send_sem.at[c, k],
            recv_sem=recv_sem.at[c, k], device_id=peer, device_id_type=MESH,
        )
        copy.start()
        return copy

    def chunk(c):
        tap, b = TAP_ORDER[c // 3], c % 3
        part = jnp.dot(
            cot_t[...],
            wide_img[tap * cols : tap * cols + pixels, b * chan : (b + 1) * chan],
            preferred_element_type=jnp.float32,
        )
        acc[c] = part.reshape(rows_size // 2, 2, pieces, SUB, chan)
        copy = send(acc.at[c, :, 1 - core], first.at[c], c, 0, core_peer)
        sent.append(copy)
        yield
        copy.wait_recv()
        work[c] = acc[c, :, core] + first[c]
        q0, nq, p0, np_ = 0, rows_size // 2, 0, pieces
        undo = []
        sem = 1
        for k, (axis, bit, members, split) in enumerate(steps):
            mine, others = mates(axis, bit, members)
            qs, ps = q0, p0
            if axis == "rows":
                nq //= members
                q0 = qs + mine * nq
            elif split:
                np_ //= members
                p0 = ps + mine * np_
                undo.append((mine, members, others))
            copies = []
            for i, (place, peer) in enumerate(others):
                sq = qs + place * nq if axis == "rows" else q0
                sp = ps + place * np_ if axis == "dp" and split else p0
                copies.append(send(
                    work.at[c, pl.ds(sq, nq), pl.ds(sp, np_)], landing[k].at[c, i],
                    c, sem, peer))
                sem += 1
            yield
            keep = (c, pl.ds(q0, nq), pl.ds(p0, np_))
            total = work[keep]
            for i, copy in enumerate(copies):
                copy.wait_recv()
                total = total + landing[k][c, i]
                if split:
                    sent.append(copy)
                else:
                    copy.wait_send()
            work[keep] = total
        fin[c, pl.ds(p0, np_)] = work[c, q0, pl.ds(p0, np_)]
        for mine, members, others in reversed(undo):
            at = fin.at[c, pl.ds(p0, np_)]
            copies = []
            for _, peer in others:
                copies.append(send(at, at, c, sem, peer))
                sem += 1
            yield
            for copy in copies:
                copy.wait_recv()
            sent.extend(copies)
            p0 = p0 - mine * np_
            np_ *= members
        store(fin.at[c], gk_hbm.at[tap * 3 + b], tap_sem.at[c])

    block = 4 * cols if rows_dev % 4 == 0 else cols

    def forward_maps(m):
        total = jnp.zeros((block, chan), jnp.float32)
        for a in range(3):
            at = pl.ds(m * block + a * cols, block)
            total += jnp.dot(wide_img[at, :], ker_ref[a], preferred_element_type=jnp.float32)
        at = pl.ds(m * block, block)
        out_ref[at, :] = total.astype(jnp.bfloat16)
        store(out_ref.at[at], out_hbm.at[at], store_sem.at[0, m])

    def backward_maps(m):
        total = jnp.zeros((block, chan), jnp.float32)
        for a in range(3):
            at = pl.ds(m * block + a * cols, block)
            for b in range(3):
                total += lax.dot_general(
                    wide_cot[at, b * chan : (b + 1) * chan],
                    ker_ref[2 - a, (2 - b) * chan : (3 - b) * chan, :],
                    (((1,), (1,)), ((), ())),
                    preferred_element_type=jnp.float32,
                )
        at = pl.ds(m * block, block)
        gin_ref[at, :] = total.astype(jnp.bfloat16)
        store(gin_ref.at[at], gin_hbm.at[at], store_sem.at[1, m])

    def backward_inputs():
        widen_rows(wide_cot, cot_ref)
        edges(wide_cot, 2)

    asides = [functools.partial(forward_maps, m) for m in range(pixels // block)]
    asides += [backward_inputs]
    asides += [functools.partial(backward_maps, m) for m in range(pixels // block)]

    stages = 2 + len(steps) + sum(1 for s in steps if s[0] == "dp" and s[3])
    when = [0, 1] + [1 + GAP * (k - 1) for k in range(2, stages)]
    chunks = [chunk(c) for c in range(9)]
    for slot in range(9 + when[-1]):
        if slot == 3:
            edges(wide_img, 0)
            loads[2].wait()
        for k in reversed(range(stages)):
            c = slot - when[k]
            if 0 <= c < 9:
                next(chunks[c], None)
        if slot >= 3 and asides:
            asides.pop(0)()
    for aside in asides:
        aside()
    for copy in halos + sent:
        copy.wait_send()
    for copy in stores:
        copy.wait()


def shards(images, kernel, cotangent):
    rows_size, groups = lax.axis_size("rows"), lax.axis_size("dp")
    batch, rows_dev, cols, chan = images.shape
    pixels = rows_dev * cols
    share = chan // rows_size
    pieces = share // SUB
    width = 3 * chan
    steps = plan(rows_size, groups, pieces)
    landing = []
    nq, np_ = rows_size // 2, pieces
    count = 1
    for axis, _, members, split in steps:
        if axis == "rows":
            nq //= members
        elif split:
            np_ //= members
        count += (members - 1) * (2 if axis == "dp" and split else 1)
        landing.append(pltpu.VMEM((9, members - 1, nq, np_, SUB, chan), jnp.float32))
    hbm = pl.BlockSpec(memory_space=pltpu.HBM)
    out, gin, gk = pl.pallas_call(
        functools.partial(body, (rows_size, groups, rows_dev, cols, chan, steps)),
        out_shape=(
            jax.ShapeDtypeStruct((pixels, chan), jnp.bfloat16),
            jax.ShapeDtypeStruct((pixels, chan), jnp.bfloat16),
            jax.ShapeDtypeStruct((9, pieces, SUB, chan), jnp.float32),
        ),
        in_specs=[hbm] * 3,
        out_specs=(hbm,) * 3,
        scratch_shapes=[
            pltpu.VMEM((pixels, chan), jnp.bfloat16),
            pltpu.VMEM((pixels, chan), jnp.bfloat16),
            pltpu.VMEM((pixels, chan), jnp.bfloat16),
            pltpu.VMEM((3, width, chan), jnp.bfloat16),
            pltpu.VMEM((pixels, chan), jnp.bfloat16),
            pltpu.VMEM(((rows_dev + 2) * cols, width), jnp.bfloat16),
            pltpu.VMEM(((rows_dev + 2) * cols, width), jnp.bfloat16),
            pltpu.VMEM((chan, pixels), jnp.bfloat16),
            pltpu.VMEM((4, cols, chan), jnp.bfloat16),
            pltpu.VMEM((9, rows_size // 2, 2, pieces, SUB, chan), jnp.float32),
            pltpu.VMEM((9, rows_size // 2, pieces, SUB, chan), jnp.float32),
            pltpu.VMEM((9, rows_size // 2, pieces, SUB, chan), jnp.float32),
            pltpu.VMEM((9, pieces, SUB, chan), jnp.float32),
            *landing,
            pltpu.SemaphoreType.DMA((3,)),
            pltpu.SemaphoreType.DMA((2, rows_dev)),
            pltpu.SemaphoreType.DMA((9,)),
            pltpu.SemaphoreType.DMA((4,)),
            pltpu.SemaphoreType.DMA((4,)),
            pltpu.SemaphoreType.DMA((9, count)),
            pltpu.SemaphoreType.DMA((9, count)),
        ],
        compiler_params=pltpu.CompilerParams(
            collective_id=0, has_side_effects=True, vmem_limit_bytes=58 * 2**20),
        cost_estimate=pl.CostEstimate(
            flops=6 * 9 * pixels * chan * chan, bytes_accessed=6 * 2**20, transcendentals=0),
    )(
        images.reshape(pixels, chan),
        kernel.reshape(3, 3 * chan, chan),
        cotangent.reshape(pixels, chan),
    )
    summed = jnp.transpose(gk.reshape(3, 3, share, chan), (0, 1, 3, 2))
    batch_total = batch * groups
    return (out.reshape(images.shape), gin.reshape(images.shape), summed / float(batch_total))


def solution(mesh):
    return jax.shard_map(
        shards,
        mesh=mesh,
        in_specs=(P("dp", "rows", None, None), P(), P("dp", "rows", None, None)),
        out_specs=(
            P("dp", "rows", None, None),
            P("dp", "rows", None, None),
            P(None, None, None, "rows"),
        ),
        check_vma=False,
    )
```

```python
import functools

import jax
import jax.numpy as jnp
from jax import lax
from jax.experimental import pallas as pl
from jax.experimental.pallas import tpu as pltpu
from jax.sharding import PartitionSpec as P

MESH = pl.DeviceIdType.MESH
SUB = 8
TAPS = [(a, b) for a in (1, 0, 2) for b in (1, 0, 2)]
GAP = 3


def bits_of(size):
    return size.bit_length() - 1


def plan(rows_size, groups, pieces):
    steps = [("rows", bit, 2, True) for bit in reversed(range(1, bits_of(rows_size)))]
    left = pieces
    for bit in range(bits_of(groups)):
        split = left > 1 and bit + 1 < bits_of(groups)
        steps.append(("dp", bit, 2, split))
        left = left // 2 if split else left
    return steps


def body(
    dims,
    img_hbm, ker_hbm, cot_hbm,
    out_hbm, gin_hbm, gk_hbm,
    out_ref, gin_ref, img_ref, ker_ref, cot_ref, wide_img, wide_cot, cot_t, halo, acc, first, work, fin, *rest,
):
    rows_size, groups, rows_dev, cols, chan, batch_total, steps = dims
    landing = rest[: len(steps)]
    load_sem, store_sem, tap_sem, halo_send, halo_recv, send_sem, recv_sem = rest[len(steps):]
    pixels = rows_dev * cols
    pieces = chan // rows_size // SUB
    r = lax.axis_index("rows")
    g = lax.axis_index("dp")
    right = lax.rem(r + 1, rows_size)
    left = lax.rem(r + rows_size - 1, rows_size)

    loads = [
        pltpu.make_async_copy(src, dst, load_sem.at[k])
        for k, (src, dst) in enumerate(
            ((img_hbm, img_ref), (cot_hbm, cot_ref), (ker_hbm, ker_ref)))
    ]
    for load in loads:
        load.start()

    def mates(axis, bit, members):
        me = r if axis == "rows" else g
        mine = lax.rem(me // (1 << bit), members)
        others = []
        for k in range(1, members):
            place = lax.rem(mine + k, members)
            others.append((place, {axis: me + (place - mine) * (1 << bit)}))
        return mine, others

    core, ((_, core_peer),) = mates("rows", 0, 2)
    barrier = pltpu.get_barrier_semaphore()
    greeted = [{"rows": right}, {"rows": left}, core_peer]
    greeted += [peer for step in steps for _, peer in mates(*step[:3])[1]]
    for peer in greeted:
        pl.semaphore_signal(barrier, inc=1, device_id=peer, device_id_type=MESH)

    column = lax.broadcasted_iota(jnp.int32, (cols, chan), 0)

    def widen(dst, slot, value):
        full = value.astype(jnp.float32)
        before = jnp.where(column == 0, 0.0, pltpu.roll(full, 1, 0))
        after = jnp.where(column == cols - 1, 0.0, pltpu.roll(full, cols - 1, 0))
        at = pl.ds(pl.multiple_of(slot * cols, cols), cols)
        dst[at, 0:chan] = before.astype(jnp.bfloat16)
        dst[at, chan : 2 * chan] = value
        dst[at, 2 * chan :] = after.astype(jnp.bfloat16)

    def widen_rows(dst, src):
        def one(i, carry):
            widen(dst, i + 1, src[pl.ds(pl.multiple_of(i * cols, cols), cols), :])
            return carry

        lax.fori_loop(0, rows_dev, one, 0)

    loads[1].wait()
    cot_t[...] = jnp.transpose(cot_ref[...])
    loads[0].wait()

    def partial(c):
        tap, b = TAPS[c]
        window = img_ref[...] if c == 0 else wide_img[
            tap * cols : tap * cols + pixels, b * chan : (b + 1) * chan]
        part = jnp.dot(cot_t[...], window, preferred_element_type=jnp.float32)
        acc[c] = part.reshape(rows_size // 2, 2, pieces, SUB, chan)

    partial(0)
    pl.semaphore_wait(barrier, len(greeted))
    halos = []
    for k, (src, at, to) in enumerate((
        (img_ref, pixels - cols, right), (img_ref, 0, left),
        (cot_ref, pixels - cols, right), (cot_ref, 0, left),
    )):
        halos.append(pltpu.make_async_remote_copy(
            src_ref=src.at[pl.ds(at, cols)], dst_ref=halo.at[k],
            send_sem=halo_send.at[k], recv_sem=halo_recv.at[k],
            device_id={"rows": to}, device_id_type=MESH,
        ))
        halos[-1].start()

    def edges(dst, k):
        halos[k].wait_recv()
        halos[k + 1].wait_recv()
        zero = jnp.zeros((cols, chan), jnp.bfloat16)
        widen(dst, 0, jnp.where(r > 0, halo[k], zero))
        widen(dst, rows_dev + 1, jnp.where(r < rows_size - 1, halo[k + 1], zero))

    sent, stores = [], []

    def store(src, dst, sem):
        stores.append(pltpu.make_async_copy(src, dst, sem))
        stores[-1].start()

    def send(src, dst, c, k, peer):
        copy = pltpu.make_async_remote_copy(
            src_ref=src, dst_ref=dst, send_sem=send_sem.at[c, k],
            recv_sem=recv_sem.at[c, k], device_id=peer, device_id_type=MESH,
        )
        copy.start()
        return copy

    def chunk(c):
        if c > 0:
            partial(c)
        copy = send(acc.at[c, :, 1 - core], first.at[c], c, 0, core_peer)
        sent.append(copy)
        yield
        copy.wait_recv()
        work[c] = acc[c, :, core] + first[c]
        q0, nq, p0, np_ = 0, rows_size // 2, 0, pieces
        undo = []
        sem = 1
        for k, (axis, bit, members, split) in enumerate(steps):
            mine, others = mates(axis, bit, members)
            qs, ps = q0, p0
            if axis == "rows":
                nq //= members
                q0 = qs + mine * nq
            elif split:
                np_ //= members
                p0 = ps + mine * np_
                undo.append((mine, members, others))
            copies = []
            for i, (place, peer) in enumerate(others):
                sq = qs + place * nq if axis == "rows" else q0
                sp = ps + place * np_ if axis == "dp" and split else p0
                copies.append(send(
                    work.at[c, pl.ds(sq, nq), pl.ds(sp, np_)], landing[k].at[c, i],
                    c, sem, peer))
                sem += 1
            yield
            keep = (c, pl.ds(q0, nq), pl.ds(p0, np_))
            total = work[keep]
            for i, copy in enumerate(copies):
                copy.wait_recv()
                total = total + landing[k][c, i]
                if split:
                    sent.append(copy)
                else:
                    copy.wait_send()
            work[keep] = total
        fin[c, pl.ds(p0, np_)] = work[c, q0, pl.ds(p0, np_)] / float(batch_total)
        for mine, members, others in reversed(undo):
            at = fin.at[c, pl.ds(p0, np_)]
            copies = []
            for _, peer in others:
                copies.append(send(at, at, c, sem, peer))
                sem += 1
            yield
            for copy in copies:
                copy.wait_recv()
            sent.extend(copies)
            p0 = p0 - mine * np_
            np_ *= members
        store(fin.at[c], gk_hbm.at[TAPS[c][0] * 3 + TAPS[c][1]], tap_sem.at[c])

    block = 4 * cols if rows_dev % 4 == 0 else cols

    def forward_maps(m):
        total = jnp.zeros((block, chan), jnp.float32)
        for a in range(3):
            at = pl.ds(m * block + a * cols, block)
            total += jnp.dot(wide_img[at, :], ker_ref[a], preferred_element_type=jnp.float32)
        at = pl.ds(m * block, block)
        out_ref[at, :] = total.astype(jnp.bfloat16)
        store(out_ref.at[at], out_hbm.at[at], store_sem.at[0, m])

    def backward_maps(m):
        total = jnp.zeros((block, chan), jnp.float32)
        for a in range(3):
            at = pl.ds(m * block + a * cols, block)
            for b in range(3):
                total += lax.dot_general(
                    wide_cot[at, b * chan : (b + 1) * chan],
                    ker_ref[2 - a, (2 - b) * chan : (3 - b) * chan, :],
                    (((1,), (1,)), ((), ())),
                    preferred_element_type=jnp.float32,
                )
        at = pl.ds(m * block, block)
        gin_ref[at, :] = total.astype(jnp.bfloat16)
        store(gin_ref.at[at], gin_hbm.at[at], store_sem.at[1, m])

    def backward_inputs():
        widen_rows(wide_cot, cot_ref)
        edges(wide_cot, 2)

    asides = [functools.partial(forward_maps, m) for m in range(pixels // block)]
    asides += [backward_inputs]
    asides += [functools.partial(backward_maps, m) for m in range(pixels // block)]

    stages = 2 + len(steps) + sum(1 for s in steps if s[0] == "dp" and s[3])
    when = [0, 1] + [1 + GAP * (k - 1) for k in range(2, stages)]
    chunks = [chunk(c) for c in range(9)]
    for slot in range(9 + when[-1]):
        if slot == 3:
            edges(wide_img, 0)
            loads[2].wait()
        for k in reversed(range(stages)):
            c = slot - when[k]
            if 0 <= c < 9:
                next(chunks[c], None)
        if slot == 0:
            widen_rows(wide_img, img_ref)
        if slot >= 3 and asides:
            asides.pop(0)()
    for aside in asides:
        aside()
    for copy in halos + sent:
        copy.wait_send()
    for copy in stores:
        copy.wait()


def shards(images, kernel, cotangent):
    rows_size, groups = lax.axis_size("rows"), lax.axis_size("dp")
    batch, rows_dev, cols, chan = images.shape
    pixels = rows_dev * cols
    share = chan // rows_size
    pieces = share // SUB
    width = 3 * chan
    steps = plan(rows_size, groups, pieces)
    landing = []
    nq, np_ = rows_size // 2, pieces
    count = 1
    for axis, _, members, split in steps:
        if axis == "rows":
            nq //= members
        elif split:
            np_ //= members
        count += (members - 1) * (2 if axis == "dp" and split else 1)
        landing.append(pltpu.VMEM((9, members - 1, nq, np_, SUB, chan), jnp.float32))
    hbm = pl.BlockSpec(memory_space=pltpu.HBM)
    out, gin, gk = pl.pallas_call(
        functools.partial(body, (rows_size, groups, rows_dev, cols, chan, batch * groups, steps)),
        out_shape=(
            jax.ShapeDtypeStruct((pixels, chan), jnp.bfloat16),
            jax.ShapeDtypeStruct((pixels, chan), jnp.bfloat16),
            jax.ShapeDtypeStruct((9, pieces, SUB, chan), jnp.float32),
        ),
        in_specs=[hbm] * 3,
        out_specs=(hbm,) * 3,
        scratch_shapes=[
            pltpu.VMEM((pixels, chan), jnp.bfloat16),
            pltpu.VMEM((pixels, chan), jnp.bfloat16),
            pltpu.VMEM((pixels, chan), jnp.bfloat16),
            pltpu.VMEM((3, width, chan), jnp.bfloat16),
            pltpu.VMEM((pixels, chan), jnp.bfloat16),
            pltpu.VMEM(((rows_dev + 2) * cols, width), jnp.bfloat16),
            pltpu.VMEM(((rows_dev + 2) * cols, width), jnp.bfloat16),
            pltpu.VMEM((chan, pixels), jnp.bfloat16),
            pltpu.VMEM((4, cols, chan), jnp.bfloat16),
            pltpu.VMEM((9, rows_size // 2, 2, pieces, SUB, chan), jnp.float32),
            pltpu.VMEM((9, rows_size // 2, pieces, SUB, chan), jnp.float32),
            pltpu.VMEM((9, rows_size // 2, pieces, SUB, chan), jnp.float32),
            pltpu.VMEM((9, pieces, SUB, chan), jnp.float32),
            *landing,
            pltpu.SemaphoreType.DMA((3,)),
            pltpu.SemaphoreType.DMA((2, rows_dev)),
            pltpu.SemaphoreType.DMA((9,)),
            pltpu.SemaphoreType.DMA((4,)),
            pltpu.SemaphoreType.DMA((4,)),
            pltpu.SemaphoreType.DMA((9, count)),
            pltpu.SemaphoreType.DMA((9, count)),
        ],
        compiler_params=pltpu.CompilerParams(
            collective_id=0, has_side_effects=True, vmem_limit_bytes=58 * 2**20),
        cost_estimate=pl.CostEstimate(
            flops=6 * 9 * pixels * chan * chan, bytes_accessed=6 * 2**20, transcendentals=0),
    )(
        images.reshape(pixels, chan),
        kernel.reshape(3, 3 * chan, chan),
        cotangent.reshape(pixels, chan),
    )
    summed = jnp.transpose(gk.reshape(3, 3, share, chan), (0, 1, 3, 2))
    return (out.reshape(images.shape), gin.reshape(images.shape), summed)


def solution(mesh):
    return jax.shard_map(
        shards,
        mesh=mesh,
        in_specs=(P("dp", "rows", None, None), P(), P("dp", "rows", None, None)),
        out_specs=(
            P("dp", "rows", None, None),
            P("dp", "rows", None, None),
            P(None, None, None, "rows"),
        ),
        check_vma=False,
    )
```
